256 devices in a mesh: patch: 16 (over y, z_hi, core), tp: 16 (over z_lo, x).
Axes of the slice: x: 4, y: 4, z: 8 (z_hi: 2, z_lo: 4; z = z_hi * 4 + z_lo), core: 2. Of those that a mesh axis runs over, the one named last changes fastest.
Arguments:
- latent: bfloat16 [4096, 3072], P('patch', 'tp'), may hold values from -25 to 25, as said below
- modulation: float32 [2, 3, 3072], replicated, may hold values from -4 to 4
- stale_kv: bfloat16 [2, 4096, 2048], P(None, 'patch', 'tp'), may hold values from -40 to 40
- w_qkv: bfloat16 [3072, 3, 2048], P(('patch', 'tp')), may hold values from -0.109375 to 0.109375
- w_out: bfloat16 [3072, 2048], P('tp', 'patch'), may hold values from -0.25 to 0.25
- q_gain: float32 [128], replicated, may hold values from 0.7 to 3
- k_gain: float32 [128], replicated, may hold values from 0.7 to 3
Outputs:
- latent_out: bfloat16 [4096, 3072], P('patch', 'tp')
- next_kv: bfloat16 [2, 4096, 2048], P(None, 'patch', 'tp')
The draws below stay inside these ranges and needn't reach their ends.
Inputs may be any that keep to these rules, and one draw needn't show every extreme that they name: latent tokens of varying scale.
All inputs are finite; a program needn't handle non-finite values.
Results may differ from the reference program's by a relative error of at most 0.03.
Values may be sent and summed in bfloat16 or wider, within the bound.
No kernel may reach another device: no remote copies, remote signals or barrier semaphores. Data moves between devices by JAX's collectives and lax.ppermute only.
A program may use at most 64 MiB of HBM per device.

```python
import jax
import jax.numpy as jnp
from jax import lax

D = 3072
HEADS = 16
HEAD_DIM = 128
HW = 2048
TOK_DEV = 256
STEPS = 2
TOKENS = 4096
N_PATCH = 16
N_TP = 16


def make_gain(key, low, high):
    return jnp.exp(jax.random.uniform(key, (HEAD_DIM,), jnp.float32, jnp.log(low), jnp.log(high)))


def draw_latent(key, part):
    key = jax.random.fold_in(key, 11)
    key_rows, key_cols, key_base = jax.random.split(key, 3)
    rows = jnp.exp(jax.random.uniform(key_rows, (TOKENS, 1), jnp.float32, jnp.log(0.3), jnp.log(3.0)))
    cols = jnp.exp(jax.random.uniform(key_cols, (1, D), jnp.float32, jnp.log(0.5), jnp.log(2.0)))
    base = jnp.clip(jax.random.normal(key_base, (TOKENS, D), jnp.float32), -4.0, 4.0)
    return (base * rows * cols).astype(jnp.bfloat16)


def draw_q_gain(key, part):
    key = jax.random.fold_in(key, 21)
    return make_gain(key, 0.7, 1.5)


def draw_k_gain(key, part):
    key = jax.random.fold_in(key, 22)
    return make_gain(key, 0.7, 1.5)


def draw_stale_kv(key, part):
    gain = draw_k_gain(key, part)
    key = jax.random.fold_in(key, 31)
    key_keys, key_vals = jax.random.split(key, 2)
    raw = jnp.clip(jax.random.normal(key_keys, (TOKENS, HEADS, HEAD_DIM), jnp.float32), -4.0, 4.0)
    vals = jnp.clip(jax.random.normal(key_vals, (TOKENS, HW), jnp.float32), -6.0, 6.0)
    normed = raw * jax.lax.rsqrt(jnp.mean(raw * raw, axis=-1, keepdims=True) + 1e-06) * gain
    keys = jnp.clip(normed, -40.0, 40.0).reshape(TOKENS, HW)
    return jnp.stack([keys, vals]).astype(jnp.bfloat16)


def levels(stream_key, extent, shards, low, largest):
    level, own = 1.0, jax.random.fold_in(stream_key, 6)
    for dim, parts in shards:
        steps = jnp.exp(jax.random.uniform(jax.random.fold_in(own, dim), (parts,), jnp.float32, low / len(shards), largest / len(shards)))
        level = level * jnp.repeat(steps, extent[dim] // parts).reshape([-1 if axis == dim else 1 for axis in range(len(extent))])
    return level


def centred(rng, shape, width, most, shards=(), kind=jnp.bfloat16):
    array = width * jax.random.normal(rng, shape, jnp.float32)
    if shards:
        array = array * levels(rng, shape, shards, -0.22, 0.18)
    return jnp.clip(array, -most, most).astype(kind)


def setup_inputs(seed: int = 0) -> dict:
    splits = jax.random.split(jax.random.key(seed), 8)
    return {
        "latent": draw_latent(jax.random.fold_in(splits[7], 71), 0),
        "modulation": centred(splits[1], (STEPS, 3, D), 1.0, 4.0, (), jnp.float32),
        "stale_kv": draw_stale_kv(jax.random.fold_in(splits[7], 71), 0),
        "w_qkv": centred(splits[3], (D, 3, HW), D ** -0.5, 0.109375, ((0, 256),)),
        "w_out": centred(splits[4], (D, HW), (HW // 4) ** -0.5, 0.25, ((0, 16), (1, 16))),
        "q_gain": draw_q_gain(jax.random.fold_in(splits[7], 71), 0),
        "k_gain": draw_k_gain(jax.random.fold_in(splits[7], 71), 0),
    }


EPS = 1e-06

def layer_norm(values):
    centre = values - lax.optimization_barrier(jnp.mean(values, axis=-1, keepdims=True))
    spread = lax.optimization_barrier(jnp.mean(centre * centre, axis=-1, keepdims=True))
    return centre * lax.rsqrt(spread + EPS)

def head_rms(values, gain):
    shaped = values.reshape(values.shape[0], -1, HEAD_DIM)
    scaled = shaped * lax.rsqrt(lax.optimization_barrier(jnp.mean(shaped * shaped, axis=-1, keepdims=True)) + EPS) * gain
    return scaled.reshape(values.shape[0], -1)

def attend(query, fresh_k, fresh_v, past_k, past_v):
    q_blocks = query.reshape(N_PATCH, TOK_DEV, HEADS, HEAD_DIM)
    owner = jnp.arange(TOKENS, dtype=jnp.int32) // TOK_DEV
    fk = fresh_k.reshape(TOKENS, HEADS, HEAD_DIM)
    fv = fresh_v.reshape(TOKENS, HEADS, HEAD_DIM)
    pk = past_k.reshape(TOKENS, HEADS, HEAD_DIM)
    pv = past_v.reshape(TOKENS, HEADS, HEAD_DIM)
    inv_root = 1.0 / HEAD_DIM ** 0.5

    def one_patch(packed):
        index, q_rows = packed
        mine = (owner == index)[:, None, None]
        keys = jnp.where(mine, fk, pk).astype(jnp.float32)
        vals = jnp.where(mine, fv, pv).astype(jnp.float32)
        scores = jnp.einsum('qhd,khd->hqk', q_rows.astype(jnp.float32), keys) * inv_root
        top = lax.optimization_barrier(jnp.max(scores, axis=-1, keepdims=True))
        weights = jnp.exp(scores - top)
        total = lax.optimization_barrier(jnp.sum(weights, axis=-1))
        mixed = jnp.einsum('hqk,khd->qhd', weights.astype(jnp.bfloat16).astype(jnp.float32), vals)
        return (mixed / jnp.transpose(total)[:, :, None]).astype(jnp.bfloat16)
    result = lax.map(one_patch, (jnp.arange(N_PATCH, dtype=jnp.int32), q_blocks))
    return result.reshape(TOKENS, HW)

def reference(latent, modulation, stale_kv, w_qkv, w_out, q_gain, k_gain):
    state = latent
    past_k = stale_kv[0]
    past_v = stale_kv[1]
    group = HW // N_TP
    flat_qkv = w_qkv.reshape(D, 3 * HW)
    for step in range(STEPS):
        wide = state.astype(jnp.float32)
        normed = (layer_norm(wide) * (1.0 + modulation[step, 1]) + modulation[step, 0]).astype(jnp.bfloat16)
        qkv = jnp.dot(normed, flat_qkv, preferred_element_type=jnp.float32).reshape(TOKENS, 3, HW)
        query = head_rms(qkv[:, 0], q_gain).astype(jnp.bfloat16)
        keys = head_rms(qkv[:, 1], k_gain).astype(jnp.bfloat16)
        values = qkv[:, 2].astype(jnp.bfloat16)
        attn = attend(query, keys, values, past_k, past_v)
        proj = jnp.zeros((TOKENS, D), jnp.float32)
        for index in range(N_TP):
            part = jnp.dot(attn[:, index * group:(index + 1) * group], jnp.transpose(w_out[:, index * group:(index + 1) * group]), preferred_element_type=jnp.float32)
            rounded = lax.optimization_barrier(part.astype(jnp.bfloat16))
            proj = proj + rounded.astype(jnp.float32)
        state = (wide + modulation[step, 2] * proj).astype(jnp.bfloat16)
        past_k = keys
        past_v = values
    return (state, jnp.stack([past_k, past_v]))
```

```python
import functools

import jax
import jax.numpy as jnp
from jax import lax
from jax.experimental import pallas as pl
from jax.experimental.pallas import tpu as pltpu
from jax.sharding import PartitionSpec as P

NY, NH, NC = 4, 2, 2
NL, NX = 4, 4
STEPS = 2
EPS = 1e-06
VMEM = 40 * 1024 * 1024
BF = jnp.bfloat16
F32 = jnp.float32


def shift(array, axis, amount):
    if axis in ("l", "x"):
        pairs = []
        for l in range(NL):
            for x in range(NX):
                to = ((l + amount) % NL, x) if axis == "l" else (l, (x + amount) % NX)
                pairs.append((l * NX + x, to[0] * NX + to[1]))
        return lax.ppermute(array, "tp", pairs)
    pairs = []
    for y in range(NY):
        for h in range(NH):
            for c in range(NC):
                to = {
                    "y": ((y + amount) % NY, h, c),
                    "h": (y, (h + amount) % NH, c),
                    "c": (y, h, (c + amount) % NC),
                }[axis]
                pairs.append(((y * NH + h) * NC + c, (to[0] * NH + to[1]) * NC + to[2]))
    return lax.ppermute(array, "patch", pairs)


def after(value, *others):
    return lax.optimization_barrier((value,) + others)[0]


def tp_of(ids, kl, kx):
    tp = ids[1]
    l, x = tp // NX, tp % NX
    return ((l + NL - kl) % NL) * NX + (x + NX - kx) % NX


def patch_of(ids, ky, kh, kc):
    patch = ids[0]
    y, h, c = patch // (NH * NC), (patch // NC) % NH, patch % NC
    return (((y + NY - ky) % NY) * NH + (h + kh) % NH) * NC + (c + kc) % NC


def call(body, outs, inputs, scratch, flops, name, smem=1):
    vm = pl.BlockSpec(memory_space=pltpu.VMEM)
    specs = [pl.BlockSpec(memory_space=pltpu.SMEM)] * smem + [vm] * (len(inputs) - smem)
    return pl.pallas_call(
        body,
        out_shape=outs,
        in_specs=specs,
        out_specs=[vm] * len(outs),
        scratch_shapes=scratch,
        compiler_params=pltpu.CompilerParams(vmem_limit_bytes=VMEM),
        cost_estimate=pl.CostEstimate(flops=flops, bytes_accessed=4 << 20, transcendentals=0),
        name=name,
    )(*inputs)


def dot(a, b, dims):
    return lax.dot_general(a, b, (dims, ((), ())), preferred_element_type=F32)


def qkv_body(step, ids, mod, x0, x1, x2, x3, w_own, w_far, qg, kg, q_out, k_out, v_out, normed, rows):
    feat, tok = x0.shape[1], x0.shape[2]
    total = feat * NL * NX
    groups = (x0, x1, x2, x3)
    acc = jnp.zeros((1, tok), F32)
    for group in groups:
        for kl in range(NL):
            acc += jnp.sum(group[kl].astype(F32), axis=0, keepdims=True)
    mean = acc / total
    acc = jnp.zeros((1, tok), F32)
    for group in groups:
        for kl in range(NL):
            centre = group[kl].astype(F32) - mean
            acc += jnp.sum(centre * centre, axis=0, keepdims=True)
    rstd = lax.rsqrt(acc / total + EPS)
    places = [(kx, kl) for kx in range(NX) for kl in range(NL)]
    rows[...] = jnp.zeros_like(rows)
    for n, (kx, kl) in enumerate(places):
        t = tp_of(ids, kl, kx)
        rows[n : n + 1, 0:feat] = mod[pl.ds((step * 3 + 1) * NL * NX + t, 1), :] + 1.0
        rows[n + 16 : n + 17, 0:feat] = mod[pl.ds(step * 3 * NL * NX + t, 1), :]
    cols = jnp.transpose(rows[...])
    for n, (kx, kl) in enumerate(places):
        t = tp_of(ids, kl, kx)
        block = (groups[kx][kl].astype(F32) - mean) * rstd
        block = block * cols[0:feat, n : n + 1] + cols[0:feat, n + 16 : n + 17]
        normed[t] = block.astype(BF)
    qkv = jnp.zeros((tok, w_own.shape[-1]), F32)
    for kc, w in enumerate((w_own, w_far)):
        for ky in range(NY):
            for kh in range(NH):
                p = patch_of(ids, ky, kh, kc)
                qkv += dot(normed[p], w[ky, kh], ((0,), (0,)))
    size = qg.shape[-1]
    for n, (gain, out) in enumerate(((qg, q_out), (kg, k_out))):
        part = qkv[:, n * size : (n + 1) * size]
        scale = lax.rsqrt(jnp.mean(part * part, axis=-1, keepdims=True) + EPS)
        out[...] = (part * scale * gain[...]).astype(BF)
    v_out[...] = qkv[:, 2 * size :].astype(BF)


def attend_body(q_ref, k_ref, v_ref, own, far, out, scores):
    size = q_ref.shape[-1]
    tok = k_ref.shape[0]
    q = q_ref[...]
    blocks = [(k_ref, v_ref)]
    for group, skip in ((own, True), (far, False)):
        for ky in range(NY):
            for kh in range(NH):
                if not (skip and ky == 0 and kh == 0):
                    blocks.append((group.at[ky, kh, 0], group.at[ky, kh, 1]))
    top = jnp.full((1, q.shape[0]), -jnp.inf, F32)
    for n, (k, _) in enumerate(blocks):
        s = dot(k[...], q, ((1,), (1,)))
        scores[n] = s
        top = jnp.maximum(top, jnp.max(s, axis=0, keepdims=True))
    inv = 1.0 / size**0.5
    total = jnp.zeros_like(top)
    mixed = jnp.zeros((size, q.shape[0]), F32)
    for n, (_, v) in enumerate(blocks):
        p = jnp.exp((scores[n] - top) * inv)
        total += jnp.sum(p, axis=0, keepdims=True)
        mixed += dot(v[...], p.astype(BF), ((0,), (0,)))
    out[...] = (mixed / total).astype(BF)


def project_body(step, ids, mod, x, a0, a1, a2, a3, w_own, w_far, out, w_all, rows):
    feat = x.shape[0]
    size = w_own.shape[-1]
    for kc, w in enumerate((w_own, w_far)):
        for ky in range(NY):
            for kh in range(NH):
                w_all[patch_of(ids, ky, kh, kc)] = w[ky, kh]
    acc = jnp.zeros(x.shape, F32)
    for kx, group in enumerate((a0, a1, a2, a3)):
        for kl in range(NL):
            acc += dot(w_all[tp_of(ids, kl, kx)], group[kl], ((1,), (0,)))
    rows[...] = jnp.zeros_like(rows)
    rows[0:1, 0:feat] = mod[pl.ds((step * 3 + 2) * NL * NX + ids[1], 1), :]
    gate = jnp.transpose(rows[...])[0:feat, 0:1]
    out[...] = (x[...].astype(F32) + gate * acc).astype(BF)


def around(array, axis, count):
    return [array] + [shift(array, axis, k) for k in range(1, count)]


def on_device(latent, modulation, stale_kv, w_qkv, w_out, q_gain, k_gain):
    feat = latent.shape[1]
    tok = latent.shape[0]
    size = q_gain.shape[0]
    n_tp = NL * NX
    ids = jnp.stack([lax.axis_index("patch"), lax.axis_index("tp")]).astype(jnp.int32)
    mod = modulation.reshape(STEPS * 3 * n_tp, feat)
    qg, kg = q_gain.reshape(1, size), k_gain.reshape(1, size)
    x = latent.T

    rows_dev = w_qkv.shape[0]
    sent = w_qkv.reshape(rows_dev, 3, n_tp, size).transpose(2, 1, 0, 3).reshape(n_tp, 3 * rows_dev, size)
    w_mine = lax.all_to_all(sent, "tp", 0, 0)
    w_mine = (
        w_mine.reshape(n_tp, 3, rows_dev, size).transpose(0, 2, 1, 3).reshape(n_tp * rows_dev, 3 * size)
    )
    bundle = jnp.concatenate([stale_kv.reshape(2 * tok, size), w_out], axis=0)

    def across(array):
        pair = jnp.stack([array, shift(array, "h", 1)])
        quad = jnp.stack(around(pair, "y", NY))
        return quad, shift(quad, "c", 1)

    def widen(array):
        return around(jnp.stack(around(array, "l", NL)), "x", NX)

    groups = widen(x)
    kv_own, kv_far = across(bundle)
    w_own, w_far = across(w_mine)

    def split(quad):
        kv = quad[:, :, : 2 * tok].reshape(NY, NH, 2, tok, size)
        return kv, quad[:, :, 2 * tok :]

    (past_own, out_own), (past_far, out_far) = split(kv_own), split(kv_far)
    for step in range(STEPS):
        if step:
            groups = widen(x)
        q, k, v = call(
            functools.partial(qkv_body, step),
            [jax.ShapeDtypeStruct((tok, size), BF)] * 3,
            [ids, mod, *groups, w_own, w_far, qg, kg],
            [pltpu.VMEM((n_tp, feat, tok), BF), pltpu.VMEM((128, 256), F32)],
            2 * tok * feat * n_tp * 3 * size,
            "qkv",
        )
        kv = jnp.stack([k, v])
        if step + 1 < STEPS:
            next_own, next_far = across(kv)
        (attn,) = call(
            attend_body,
            [jax.ShapeDtypeStruct((size, tok), BF)],
            [q, k, v, past_own, past_far],
            [pltpu.VMEM((NY * NH * NC, tok, tok), F32)],
            4 * tok * tok * NY * NH * NC * size,
            "attend",
            smem=0,
        )
        (x,) = call(
            functools.partial(project_body, step),
            [jax.ShapeDtypeStruct((feat, tok), BF)],
            [ids, mod, x, *widen(attn), out_own, out_far],
            [pltpu.VMEM((NY * NH * NC, feat, size), BF), pltpu.VMEM((128, 256), F32)],
            2 * tok * feat * n_tp * size,
            "project",
        )
        if step + 1 < STEPS:
            past_own, past_far = next_own, next_far
    return x.T, kv


def solution(mesh):
    in_specs = (
        P("patch", "tp"),
        P(),
        P(None, "patch", "tp"),
        P(("patch", "tp"), None, None),
        P("tp", "patch"),
        P(),
        P(),
    )
    out_specs = (P("patch", "tp"), P(None, "patch", "tp"))
    return jax.shard_map(on_device, mesh=mesh, in_specs=in_specs, out_specs=out_specs, check_vma=False)
```

```python
import functools

import jax
import jax.numpy as jnp
from jax import lax
from jax.experimental import pallas as pl
from jax.experimental.pallas import tpu as pltpu
from jax.sharding import PartitionSpec as P

NY, NH, NC = 4, 2, 2
NL, NX = 4, 4
N_TP = NL * NX
N_PATCH = NY * NH * NC
STEPS = 2
EPS = 1e-06
BF = jnp.bfloat16
F32 = jnp.float32
LOG2E = 1.4426950408889634


def shift(array, axis, amount):
    if axis in ("l", "x"):
        pairs = []
        for l in range(NL):
            for x in range(NX):
                to = ((l + amount) % NL, x) if axis == "l" else (l, (x + amount) % NX)
                pairs.append((l * NX + x, to[0] * NX + to[1]))
        return lax.ppermute(array, "tp", pairs)
    pairs = []
    for y in range(NY):
        for h in range(NH):
            for c in range(NC):
                to = {
                    "y": ((y + amount) % NY, h, c),
                    "h": (y, (h + amount) % NH, c),
                    "c": (y, h, (c + amount) % NC),
                }[axis]
                pairs.append(((y * NH + h) * NC + c, (to[0] * NH + to[1]) * NC + to[2]))
    return lax.ppermute(array, "patch", pairs)


def shifts(array, axis, count):
    return [shift(array, axis, k) for k in range(1, count)]


def sync(*trees):
    leaves, kind = jax.tree.flatten(trees)
    return jax.tree.unflatten(kind, lax.optimization_barrier(tuple(leaves)))


def call(body, outs, inputs, scratch, cost, room, name):
    vector = pl.BlockSpec(memory_space=pltpu.VMEM)
    return pl.pallas_call(
        body,
        out_shape=outs,
        in_specs=[pl.BlockSpec(memory_space=pltpu.SMEM)] + [vector] * (len(inputs) - 1),
        out_specs=[vector] * len(outs),
        scratch_shapes=scratch,
        compiler_params=pltpu.CompilerParams(vmem_limit_bytes=room << 20),
        cost_estimate=pl.CostEstimate(flops=1 << 20, bytes_accessed=cost << 20, transcendentals=0),
        name=name,
    )(*inputs)


def dot(a, b, dims):
    return lax.dot_general(a, b, (dims, ((), ())), preferred_element_type=F32)


def blocks(refs, table):
    return [(ref, i, first + i) for ref, first in zip(refs, table) for i in range(ref.shape[0])]


def tp_of(ids, n):
    l, x = ids[1] // NX, ids[1] % NX
    return ((l + NL - n % NL) % NL) * NX + (x + NX - n // NL) % NX


def patch_of(ids, n):
    patch = ids[0]
    y, h, c = patch // (NH * NC), (patch // NC) % NH, patch % NC
    ky, kh, kc = (n // NH) % NY, n % NH, n // (NH * NY)
    return (((y + NY - ky) % NY) * NH + (h + kh) % NH) * NC + (c + kc) % NC


def qkv_body(step, x_table, w_table, ids, mod, qg, kg, *refs):
    n_x, n_w = len(x_table), len(w_table)
    x_in, w_in = blocks(refs[:n_x], x_table), blocks(refs[n_x : n_x + n_w], w_table)
    q_out, kv_out, normed, rows = refs[n_x + n_w :]
    feat, tok = normed.shape[1:]
    total = feat * N_TP
    rows[...] = jnp.zeros_like(rows)
    for n in range(N_TP):
        t = tp_of(ids, n)
        rows[n : n + 1, 0:feat] = mod[pl.ds((step * 3 + 1) * N_TP + t, 1), :] + 1.0
        rows[n + 16 : n + 17, 0:feat] = mod[pl.ds(step * 3 * N_TP + t, 1), :]
    cols = jnp.transpose(rows[...])
    mean = jnp.zeros((1, tok), F32)
    for ref, i, n in x_in:
        mean += jnp.sum(ref[i].astype(F32), axis=0, keepdims=True)
    mean = mean / total
    spread = jnp.zeros((1, tok), F32)
    for ref, i, n in x_in:
        centre = ref[i].astype(F32) - mean
        spread += jnp.sum(centre * centre, axis=0, keepdims=True)
    rstd = lax.rsqrt(spread / total + EPS)
    for ref, i, n in x_in:
        block = (ref[i].astype(F32) - mean) * rstd
        block = block * cols[0:feat, n : n + 1] + cols[0:feat, n + 16 : n + 17]
        normed[tp_of(ids, n)] = block.astype(BF)
    size = qg.shape[-1]
    qkv = jnp.zeros((tok, 3 * size), F32)
    for ref, i, n in w_in:
        qkv += dot(normed[patch_of(ids, n)], ref[i, :, 0 : 3 * size], ((0,), (0,)))
    for n, (gain, out) in enumerate(((qg, q_out), (kg, kv_out.at[0:tok]))):
        one = qkv[:, n * size : (n + 1) * size]
        scale = lax.rsqrt(jnp.mean(one * one, axis=-1, keepdims=True) + EPS)
        out[...] = (one * scale * gain[...]).astype(BF)
    kv_out[tok:] = qkv[:, 2 * size :].astype(BF)


def attend_body(table, ids, q_ref, kv_ref, *refs):
    past, (out, scores) = refs[: len(table)], refs[len(table) :]
    tok, size = q_ref.shape
    keys = [(kv_ref.at[0:tok], kv_ref.at[tok:])]
    for ref, i, n in blocks(past, table):
        if n:
            keys.append((ref.at[i, 0:tok], ref.at[i, tok : 2 * tok]))
    q = q_ref[...]
    top = jnp.full((1, tok), -jnp.inf, F32)
    for n, (k, _) in enumerate(keys):
        part = dot(k[...], q, ((1,), (1,)))
        scores[n] = part
        top = jnp.maximum(top, jnp.max(part, axis=0, keepdims=True))
    inv = LOG2E / size**0.5
    total = jnp.zeros((1, tok), F32)
    mixed = jnp.zeros((size, tok), F32)
    for n, (_, v) in enumerate(keys):
        p = jnp.exp2((scores[n] - top) * inv)
        total += jnp.sum(p, axis=0, keepdims=True)
        mixed += dot(v[...], p.astype(BF), ((0,), (0,)))
    out[...] = (mixed / total).astype(BF)


def arrange_body(table, ids, *refs):
    weights, out = refs[:-1], refs[-1]
    size = out.shape[1] // NL
    feat = out.shape[0] // NX
    l, x = ids[1] // NX, ids[1] % NX
    for ref, i, n in blocks(weights, table):
        patch = patch_of(ids, n)
        k = (patch % NX + NX - x) % NX
        kl = (l + NL - patch // NX) % NL
        rows = pl.ds(pl.multiple_of(k * feat, feat), feat)
        lanes = pl.ds(pl.multiple_of(kl * size, size), size)
        out[rows, lanes] = ref[i, :, 3 * size :]


def partial_body(ids, weights, *refs):
    attn, outs, mixed = refs[:NL], refs[NL:-1], refs[-1]
    size, feat = attn[0].shape[0], outs[0].shape[0]
    for n, part in enumerate(attn):
        mixed[n * size : (n + 1) * size] = part[...]
    acc = dot(weights[...], mixed[...], ((1,), (0,)))
    for n, out in enumerate(outs):
        out[...] = acc[n * feat : (n + 1) * feat].astype(out.dtype)


def update_body(step, ids, mod, x, own, *refs):
    came, (out, rows) = refs[:-2], refs[-2:]
    feat = x.shape[0]
    rows[...] = jnp.zeros_like(rows)
    rows[0:1, 0:feat] = mod[pl.ds((step * 3 + 2) * N_TP + ids[1], 1), :]
    gate = jnp.transpose(rows[...])[0:feat, 0:1]
    acc = own[...]
    for part in came:
        acc += part[...].astype(F32)
    out[...] = (x[...].astype(F32) + gate * acc).astype(BF)


def swap(array):
    pairs = []
    for y in range(NY):
        for m in range(NH * NC):
            for l in range(NL):
                for x in range(NX):
                    here = (y * NX + m) * N_TP + l * NX + x
                    pairs.append((here, (y * NX + x) * N_TP + l * NX + m))
    return lax.ppermute(array, ("patch", "tp"), pairs)


def on_device(latent, modulation, stale_kv, w_qkv, w_out, q_gain, k_gain):
    tok, feat = latent.shape
    size = q_gain.shape[0]
    ids = jnp.stack([lax.axis_index("patch"), lax.axis_index("tp")]).astype(jnp.int32)
    mod = modulation.reshape(STEPS * 3 * N_TP, feat)
    qg, kg = q_gain.reshape(1, size), k_gain.reshape(1, size)
    x = latent.T

    def shape(*dims):
        return jax.ShapeDtypeStruct(dims, BF)

    rows_dev = w_qkv.shape[0]
    sent = w_qkv.reshape(rows_dev, 3, N_TP, size).transpose(2, 1, 0, 3).reshape(N_TP, 3 * rows_dev, size)
    cache = stale_kv.reshape(2 * tok, size)
    w_mine = lax.all_to_all(sent, "tp", 0, 0)
    x_l = shifts(x, "l", NL)
    b_h = shift(cache, "h", 1)
    w_back = swap(w_out)
    x, x_l, cache, b_h, w_back, w_mine, ids, mod = sync(x, x_l, cache, b_h, w_back, w_mine, ids, mod)
    w_mine = w_mine.reshape(N_TP, 3, rows_dev, size).transpose(0, 2, 1, 3).reshape(N_TP * rows_dev, 3 * size)
    w_mine = jnp.concatenate([w_mine, w_back], axis=1)
    w_h = shift(w_mine, "h", 1)
    x_four = jnp.stack([x] + x_l)
    x_up, x_down = shift(x_four, "x", 1), shift(x_four, "x", 3)
    b_pair = jnp.stack([cache, b_h])
    b_up, b_down = shift(b_pair, "y", 1), shift(b_pair, "y", 3)
    w_h, x_up, x_down, b_up, b_down = sync(w_h, x_up, x_down, b_up, b_down)
    w_pair = jnp.stack([w_mine, w_h])
    w_quad = [w_pair] + shifts(w_pair, "y", NY)
    x_far = [shift(x_up[: NL // 2], "x", 1), shift(x_down[NL // 2 :], "x", 3)]
    w_quad, x_far, b_up, b_down = sync(w_quad, x_far, b_up, b_down)
    w_c = [shift(piece, "c", 1) for piece in w_quad]
    b_far = [shift(b_up[:1], "y", 1), shift(b_down[1:], "y", 3)]
    b_quad = [jnp.concatenate([b_pair, b_up, *b_far, b_down])]
    past = b_quad + [shift(b_quad[0], "c", 1)]
    past_table = [0, NY * NH]
    weights, w_table = w_quad + w_c, [NH * k for k in range(NC * NY)]
    groups, x_table = [x_four, x_up, x_down] + x_far, [0, NL, 3 * NL, 2 * NL, 2 * NL + NL // 2]
    for step in range(STEPS):
        last = step + 1 == STEPS
        q, kv = call(
            functools.partial(qkv_body, step, x_table, w_table),
            [shape(tok, size), shape(2 * tok, size)],
            [ids, mod, qg, kg, *groups, *weights],
            [pltpu.VMEM((N_TP, feat, tok), BF), pltpu.VMEM((128, 256), F32)],
            16,
            12,
            "qkv",
        )
        (attn,) = call(
            functools.partial(attend_body, past_table),
            [shape(size, tok)],
            [ids, q, kv, *past],
            [pltpu.VMEM((N_PATCH, tok, tok), F32)],
            8,
            12,
            "attend",
        )
        if not step:
            (w_all,) = call(
                functools.partial(arrange_body, w_table),
                [shape(NX * feat, NL * size)],
                [ids, *weights],
                [],
                3,
                8,
                "arrange",
            )
        came = shifts(attn, "l", NL)
        came, w_all = sync(came, w_all)
        own, *parts = call(
            partial_body,
            [jax.ShapeDtypeStruct((feat, tok), F32)] + [shape(feat, tok)] * (NX - 1),
            [ids, w_all, attn, *came],
            [pltpu.VMEM((NL * size, tok), BF)],
            2,
            8,
            "partial",
        )
        parts, kv_own = sync(parts, kv)
        sums = [shift(part, "x", k + 1) for k, part in enumerate(parts)]
        if not last:
            kv_h = shift(kv_own, "h", 1)
        (x,) = call(
            functools.partial(update_body, step),
            [shape(feat, tok)],
            [ids, mod, x, own, *sums],
            [pltpu.VMEM((128, 256), F32)],
            1,
            4,
            "update",
        )
        if last:
            break
        x, kv_h, kv_own = sync(x, kv_h, kv_own)
        x_l = shifts(x, "l", NL)
        kv_pair = jnp.stack([kv_own, kv_h])
        kv_up, kv_down = shift(kv_pair, "y", 1), shift(kv_pair, "y", 3)
        x_l, kv_up, kv_down = sync(x_l, kv_up, kv_down)
        x_four = jnp.stack([x] + x_l)
        groups, x_table = [x_four] + shifts(x_four, "x", NX), [NL * k for k in range(NX)]
        kv_far = [shift(kv_up[:1], "y", 1), shift(kv_down[1:], "y", 3)]
        groups, kv_far = sync(groups, kv_far)
        quad = [jnp.concatenate([kv_pair, kv_up, *kv_far, kv_down])]
        past = quad + [shift(quad[0], "c", 1)]
    return x.T, kv.reshape(2, tok, size)


def solution(mesh):
    in_specs = (
        P("patch", "tp"),
        P(),
        P(None, "patch", "tp"),
        P(("patch", "tp"), None, None),
        P("tp", "patch"),
        P(),
        P(),
    )
    out_specs = (P("patch", "tp"), P(None, "patch", "tp"))
    return jax.shard_map(on_device, mesh=mesh, in_specs=in_specs, out_specs=out_specs, check_vma=False)
```

```python
import functools

import jax
import jax.numpy as jnp
from jax import lax
from jax.experimental import pallas as pl
from jax.experimental.pallas import tpu as pltpu
from jax.sharding import PartitionSpec as P

NY, NH, NC = 4, 2, 2
NL, NX = 4, 4
N_TP = NL * NX
N_PATCH = NY * NH * NC
STEPS = 2
EPS = 1e-06
BF = jnp.bfloat16
F32 = jnp.float32
LOG2E = 1.4426950408889634


def shift(array, axis, amount):
    if axis in ("l", "x"):
        pairs = []
        for l in range(NL):
            for x in range(NX):
                to = ((l + amount) % NL, x) if axis == "l" else (l, (x + amount) % NX)
                pairs.append((l * NX + x, to[0] * NX + to[1]))
        return lax.ppermute(array, "tp", pairs)
    pairs = []
    for y in range(NY):
        for h in range(NH):
            for c in range(NC):
                to = {
                    "y": ((y + amount) % NY, h, c),
                    "h": (y, (h + amount) % NH, c),
                    "c": (y, h, (c + amount) % NC),
                }[axis]
                pairs.append(((y * NH + h) * NC + c, (to[0] * NH + to[1]) * NC + to[2]))
    return lax.ppermute(array, "patch", pairs)


def shifts(array, axis, count):
    return [shift(array, axis, k) for k in range(1, count)]


def sync(*trees):
    leaves, kind = jax.tree.flatten(trees)
    return jax.tree.unflatten(kind, lax.optimization_barrier(tuple(leaves)))


def call(body, outs, inputs, scratch, cost, room, name):
    vector = pl.BlockSpec(memory_space=pltpu.VMEM)
    return pl.pallas_call(
        body,
        out_shape=outs,
        in_specs=[pl.BlockSpec(memory_space=pltpu.SMEM)] + [vector] * (len(inputs) - 1),
        out_specs=[vector] * len(outs),
        scratch_shapes=scratch,
        compiler_params=pltpu.CompilerParams(vmem_limit_bytes=room << 20),
        cost_estimate=pl.CostEstimate(flops=1 << 20, bytes_accessed=cost << 20, transcendentals=0),
        name=name,
    )(*inputs)


def dot(a, b, dims):
    return lax.dot_general(a, b, (dims, ((), ())), preferred_element_type=F32)


def blocks(refs, table):
    return [(ref, i, first + i) for ref, first in zip(refs, table) for i in range(ref.shape[0])]


def tp_of(ids, n):
    l, x = ids[1] // NX, ids[1] % NX
    return ((l + NL - n % NL) % NL) * NX + (x + NX - n // NL) % NX


def patch_of(ids, n):
    patch = ids[0]
    y, h, c = patch // (NH * NC), (patch // NC) % NH, patch % NC
    ky, kh, kc = (n // NH) % NY, n % NH, n // (NH * NY)
    return (((y + NY - ky) % NY) * NH + (h + kh) % NH) * NC + (c + kc) % NC


def norm_body(step, ids, mod, *refs):
    groups, (normed, rows) = refs[:NX], refs[NX:]
    feat, tok = normed.shape[1:]
    total = feat * N_TP
    places = blocks(groups, [NL * k for k in range(NX)])
    rows[...] = jnp.zeros_like(rows)
    for n in range(N_TP):
        t = tp_of(ids, n)
        rows[n : n + 1, 0:feat] = mod[pl.ds((step * 3 + 1) * N_TP + t, 1), :] + 1.0
        rows[n + 16 : n + 17, 0:feat] = mod[pl.ds(step * 3 * N_TP + t, 1), :]
    cols = jnp.transpose(rows[...])
    mean = jnp.zeros((1, tok), F32)
    for ref, i, n in places:
        mean += jnp.sum(ref[i].astype(F32), axis=0, keepdims=True)
    mean = mean / total
    spread = jnp.zeros((1, tok), F32)
    for ref, i, n in places:
        centre = ref[i].astype(F32) - mean
        spread += jnp.sum(centre * centre, axis=0, keepdims=True)
    rstd = lax.rsqrt(spread / total + EPS)
    for ref, i, n in places:
        block = (ref[i].astype(F32) - mean) * rstd
        block = block * cols[0:feat, n : n + 1] + cols[0:feat, n + 16 : n + 17]
        normed[tp_of(ids, n)] = block.astype(BF)


def qkv_body(table, ids, normed, qg, kg, *refs):
    weights, (kv_out, near) = refs[: len(table)], refs[len(table) :]
    tok, size = normed.shape[2], qg.shape[-1]
    qkv = jnp.zeros((tok, 3 * size), F32)
    for ref, i, n in blocks(weights, table):
        qkv += dot(normed[patch_of(ids, n)], ref[i, :, 0 : 3 * size], ((0,), (0,)))
    for n, gain in enumerate((qg, kg)):
        one = qkv[:, n * size : (n + 1) * size]
        scale = lax.rsqrt(jnp.mean(one * one, axis=-1, keepdims=True) + EPS)
        near[n * tok : (n + 1) * tok] = (one * scale * gain[...]).astype(BF)
    near[2 * tok :] = qkv[:, 2 * size :].astype(BF)
    kv_out[...] = near[tok:]


def attend_body(ids, near, past, out, scores):
    tok, size = near.shape[0] // 3, near.shape[1]

    def block(n, rows):
        own = near[tok + rows.start : tok + rows.stop]
        return jnp.where(ids[0] == n, own, past[n, rows])

    q = near[0:tok]
    top = jnp.full((1, tok), -jnp.inf, F32)
    for n in range(N_PATCH):
        part = dot(block(n, slice(0, tok)), q, ((1,), (1,)))
        scores[n] = part
        top = jnp.maximum(top, jnp.max(part, axis=0, keepdims=True))
    inv = LOG2E / size**0.5
    total = jnp.zeros((1, tok), F32)
    mixed = jnp.zeros((size, tok), F32)
    for n in range(N_PATCH):
        p = jnp.exp2((scores[n] - top) * inv)
        total += jnp.sum(p, axis=0, keepdims=True)
        mixed += dot(block(n, slice(tok, 2 * tok)), p.astype(BF), ((0,), (0,)))
    out[...] = (mixed / total).astype(BF)


def arrange_body(table, ids, *refs):
    weights, out = refs[:-1], refs[-1]
    size = out.shape[1] // NL
    feat = out.shape[0] // NX
    l, x = ids[1] // NX, ids[1] % NX
    for ref, i, n in blocks(weights, table):
        patch = patch_of(ids, n)
        k = (patch % NX + NX - x) % NX
        kl = (l + NL - patch // NX) % NL
        rows = pl.ds(pl.multiple_of(k * feat, feat), feat)
        lanes = pl.ds(pl.multiple_of(kl * size, size), size)
        out[rows, lanes] = ref[i, :, 3 * size :]


def partial_body(ids, weights, *refs):
    attn, outs, mixed = refs[:NL], refs[NL:-1], refs[-1]
    size, feat = attn[0].shape[0], outs[0].shape[0]
    for n, part in enumerate(attn):
        mixed[n * size : (n + 1) * size] = part[...]
    acc = dot(weights[...], mixed[...], ((1,), (0,)))
    for n, out in enumerate(outs):
        out[...] = acc[n * feat : (n + 1) * feat].astype(out.dtype)


def update_body(step, ids, mod, x, own, *refs):
    came, (out, rows) = refs[:-2], refs[-2:]
    feat = x.shape[0]
    rows[...] = jnp.zeros_like(rows)
    rows[0:1, 0:feat] = mod[pl.ds((step * 3 + 2) * N_TP + ids[1], 1), :]
    gate = jnp.transpose(rows[...])[0:feat, 0:1]
    acc = own[...]
    for part in came:
        acc += part[...].astype(F32)
    out[...] = (x[...].astype(F32) + gate * acc).astype(BF)


def swap(array):
    pairs = []
    for y in range(NY):
        for m in range(NH * NC):
            for l in range(NL):
                for x in range(NX):
                    here = (y * NX + m) * N_TP + l * NX + x
                    pairs.append((here, (y * NX + x) * N_TP + l * NX + m))
    return lax.ppermute(array, ("patch", "tp"), pairs)


def on_device(latent, modulation, stale_kv, w_qkv, w_out, q_gain, k_gain):
    tok, feat = latent.shape
    size = q_gain.shape[0]
    ids = jnp.stack([lax.axis_index("patch"), lax.axis_index("tp")]).astype(jnp.int32)
    mod = modulation.reshape(STEPS * 3 * N_TP, feat)
    qg, kg = q_gain.reshape(1, size), k_gain.reshape(1, size)
    x = latent.T

    def shape(*dims):
        return jax.ShapeDtypeStruct(dims, BF)

    def norm(step, groups):
        return call(
            functools.partial(norm_body, step),
            [shape(N_TP, feat, tok)],
            [ids, mod, *groups],
            [pltpu.VMEM((128, 256), F32)],
            4,
            8,
            "norm",
        )[0]

    rows_dev = w_qkv.shape[0]
    sent = w_qkv.reshape(rows_dev, 3, N_TP, size).transpose(2, 1, 0, 3).reshape(N_TP, 3 * rows_dev, size)
    cache = stale_kv.reshape(2 * tok, size)
    w_mine = lax.all_to_all(sent, "tp", 0, 0)
    x_l = shifts(x, "l", NL)
    cache_all = lax.all_gather(cache, "patch")
    w_back = swap(w_out)
    x, x_l, w_back, w_mine, ids, mod = sync(x, x_l, w_back, w_mine, ids, mod)
    w_mine = w_mine.reshape(N_TP, 3, rows_dev, size).transpose(0, 2, 1, 3).reshape(N_TP * rows_dev, 3 * size)
    w_mine = jnp.concatenate([w_mine, w_back], axis=1)
    w_h = shift(w_mine, "h", 1)
    x_four = jnp.stack([x] + x_l)
    x_up, x_down = shift(x_four, "x", 1), shift(x_four, "x", 3)
    w_h, x_up, x_down = sync(w_h, x_up, x_down)
    w_pair = jnp.stack([w_mine, w_h])
    w_quad = [w_pair] + shifts(w_pair, "y", NY)
    x_far = shift(x_four, "x", 2)
    w_c = [shift(piece, "c", 1) for piece in w_quad]
    normed = norm(0, [x_four, x_up, x_far, x_down])
    w_c, w_quad, normed = sync(w_c, w_quad, normed)
    past = cache_all
    weights, w_table = w_quad + w_c, [NH * k for k in range(NC * NY)]
    for step in range(STEPS):
        last = step + 1 == STEPS
        kv, near = call(
            functools.partial(qkv_body, w_table),
            [shape(2 * tok, size), shape(3 * tok, size)],
            [ids, normed, qg, kg, *weights],
            [],
            16,
            8,
            "qkv",
        )
        if not last:
            kv_all = lax.all_gather(kv, "patch")
        (attn,) = call(
            attend_body,
            [shape(size, tok)],
            [ids, near, past],
            [pltpu.VMEM((N_PATCH, tok, tok), F32)],
            8,
            12,
            "attend",
        )
        if not step:
            (w_all,) = call(
                functools.partial(arrange_body, w_table),
                [shape(NX * feat, NL * size)],
                [ids, *weights],
                [],
                3,
                8,
                "arrange",
            )
        came = shifts(attn, "l", NL)
        came, w_all = sync(came, w_all)
        own, *parts = call(
            partial_body,
            [jax.ShapeDtypeStruct((feat, tok), F32)] + [shape(feat, tok)] * (NX - 1),
            [ids, w_all, attn, *came],
            [pltpu.VMEM((NL * size, tok), BF)],
            2,
            8,
            "partial",
        )
        sums = [shift(part, "x", k + 1) for k, part in enumerate(parts)]
        (x,) = call(
            functools.partial(update_body, step),
            [shape(feat, tok)],
            [ids, mod, x, own, *sums],
            [pltpu.VMEM((128, 256), F32)],
            1,
            4,
            "update",
        )
        if last:
            break
        x_l = shifts(x, "l", NL)
        x_four = jnp.stack([x] + x_l)
        groups = [x_four] + shifts(x_four, "x", NX)
        normed = norm(step + 1, groups)
        past = kv_all
    return x.T, kv.reshape(2, tok, size)


def solution(mesh):
    in_specs = (
        P("patch", "tp"),
        P(),
        P(None, "patch", "tp"),
        P(("patch", "tp"), None, None),
        P("tp", "patch"),
        P(),
        P(),
    )
    out_specs = (P("patch", "tp"), P(None, "patch", "tp"))
    return jax.shard_map(on_device, mesh=mesh, in_specs=in_specs, out_specs=out_specs, check_vma=False)
```

```python
import functools

import jax
import jax.numpy as jnp
from jax import lax
from jax.experimental import pallas as pl
from jax.experimental.pallas import tpu as pltpu
from jax.sharding import PartitionSpec as P

NY, NH, NC = 4, 2, 2
NL, NX = 4, 4
N_TP = NL * NX
N_PATCH = NY * NH * NC
STEPS = 2
EPS = 1e-06
BF = jnp.bfloat16
F32 = jnp.float32
LOG2E = 1.4426950408889634


def shift(array, axis, amount):
    if axis in ("l", "x"):
        pairs = []
        for l in range(NL):
            for x in range(NX):
                to = ((l + amount) % NL, x) if axis == "l" else (l, (x + amount) % NX)
                pairs.append((l * NX + x, to[0] * NX + to[1]))
        return lax.ppermute(array, "tp", pairs)
    pairs = []
    for y in range(NY):
        for h in range(NH):
            for c in range(NC):
                to = {
                    "y": ((y + amount) % NY, h, c),
                    "h": (y, (h + amount) % NH, c),
                    "c": (y, h, (c + amount) % NC),
                }[axis]
                pairs.append(((y * NH + h) * NC + c, (to[0] * NH + to[1]) * NC + to[2]))
    return lax.ppermute(array, "patch", pairs)


def shifts(array, axis, count):
    return [shift(array, axis, k) for k in range(1, count)]


def sync(*trees):
    leaves, kind = jax.tree.flatten(trees)
    return jax.tree.unflatten(kind, lax.optimization_barrier(tuple(leaves)))


def call(body, outs, inputs, scratch, cost, room, name):
    vector = pl.BlockSpec(memory_space=pltpu.VMEM)
    return pl.pallas_call(
        body,
        out_shape=outs,
        in_specs=[pl.BlockSpec(memory_space=pltpu.SMEM)] + [vector] * (len(inputs) - 1),
        out_specs=[vector] * len(outs),
        scratch_shapes=scratch,
        compiler_params=pltpu.CompilerParams(vmem_limit_bytes=room << 20),
        cost_estimate=pl.CostEstimate(flops=1 << 20, bytes_accessed=cost << 20, transcendentals=0),
        name=name,
    )(*inputs)


def dot(a, b, dims):
    return lax.dot_general(a, b, (dims, ((), ())), preferred_element_type=F32)


def blocks(refs, table):
    return [(ref, i, first + i) for ref, first in zip(refs, table) for i in range(ref.shape[0])]


def tp_of(ids, n):
    l, x = ids[1] // NX, ids[1] % NX
    return ((l + NL - n % NL) % NL) * NX + (x + NX - n // NL) % NX


def patch_of(ids, n):
    patch = ids[0]
    y, h, c = patch // (NH * NC), (patch // NC) % NH, patch % NC
    ky, kh, kc = (n // NH) % NY, n % NH, n // (NH * NY)
    return (((y + NY - ky) % NY) * NH + (h + kh) % NH) * NC + (c + kc) % NC


def norm_body(step, ids, mod, *refs):
    groups, (normed, rows) = refs[:NX], refs[NX:]
    feat, tok = normed.shape[1:]
    total = feat * N_TP
    places = blocks(groups, [NL * k for k in range(NX)])
    rows[...] = jnp.zeros_like(rows)
    for n in range(N_TP):
        t = tp_of(ids, n)
        rows[n : n + 1, 0:feat] = mod[pl.ds((step * 3 + 1) * N_TP + t, 1), :] + 1.0
        rows[n + 16 : n + 17, 0:feat] = mod[pl.ds(step * 3 * N_TP + t, 1), :]
    cols = jnp.transpose(rows[...])
    mean = jnp.zeros((1, tok), F32)
    for ref, i, n in places:
        mean += jnp.sum(ref[i].astype(F32), axis=0, keepdims=True)
    mean = mean / total
    spread = jnp.zeros((1, tok), F32)
    for ref, i, n in places:
        centre = ref[i].astype(F32) - mean
        spread += jnp.sum(centre * centre, axis=0, keepdims=True)
    rstd = lax.rsqrt(spread / total + EPS)
    for ref, i, n in places:
        block = (ref[i].astype(F32) - mean) * rstd
        block = block * cols[0:feat, n : n + 1] + cols[0:feat, n + 16 : n + 17]
        normed[tp_of(ids, n)] = block.astype(BF)


def qkv_body(table, ids, normed, qg, kg, *refs):
    weights, (kv_out, near) = refs[: len(table)], refs[len(table) :]
    tok, size = normed.shape[2], qg.shape[-1]
    qkv = jnp.zeros((tok, 3 * size), F32)
    for ref, i, n in blocks(weights, table):
        qkv += dot(normed[patch_of(ids, n)], ref[i, :, 0 : 3 * size], ((0,), (0,)))
    for n, gain in enumerate((qg, kg)):
        one = qkv[:, n * size : (n + 1) * size]
        scale = lax.rsqrt(jnp.mean(one * one, axis=-1, keepdims=True) + EPS)
        near[n * tok : (n + 1) * tok] = (one * scale * gain[...]).astype(BF)
    near[2 * tok :] = qkv[:, 2 * size :].astype(BF)
    kv_out[...] = near[tok:]


def attend_body(ids, near, past, out, scores):
    tok, size = near.shape[0] // 3, near.shape[1]

    def block(n, rows):
        own = near[tok + rows.start : tok + rows.stop]
        return jnp.where(ids[0] == n, own, past[n, rows])

    q = near[0:tok]
    top = jnp.full((1, tok), -jnp.inf, F32)
    for n in range(N_PATCH):
        part = dot(block(n, slice(0, tok)), q, ((1,), (1,)))
        scores[n] = part
        top = jnp.maximum(top, jnp.max(part, axis=0, keepdims=True))
    inv = LOG2E / size**0.5
    total = jnp.zeros((1, tok), F32)
    mixed = jnp.zeros((size, tok), F32)
    for n in range(N_PATCH):
        p = jnp.exp2((scores[n] - top) * inv)
        total += jnp.sum(p, axis=0, keepdims=True)
        mixed += dot(block(n, slice(tok, 2 * tok)), p.astype(BF), ((0,), (0,)))
    out[...] = (mixed / total).astype(BF)


def arrange_body(table, ids, *refs):
    weights, out = refs[:-1], refs[-1]
    size = out.shape[1] // NL
    feat = out.shape[0] // NX
    l, x = ids[1] // NX, ids[1] % NX
    for ref, i, n in blocks(weights, table):
        patch = patch_of(ids, n)
        k = (patch % NX + NX - x) % NX
        kl = (l + NL - patch // NX) % NL
        rows = pl.ds(pl.multiple_of(k * feat, feat), feat)
        lanes = pl.ds(pl.multiple_of(kl * size, size), size)
        out[rows, lanes] = ref[i, :, 3 * size :]


def partial_body(ids, weights, *refs):
    attn, outs, mixed = refs[:NL], refs[NL:-1], refs[-1]
    size, feat = attn[0].shape[0], outs[0].shape[0]
    for n, part in enumerate(attn):
        mixed[n * size : (n + 1) * size] = part[...]
    acc = dot(weights[...], mixed[...], ((1,), (0,)))
    for n, out in enumerate(outs):
        out[...] = acc[n * feat : (n + 1) * feat].astype(out.dtype)


def update_body(step, ids, mod, x, own, *refs):
    came, (out, rows) = refs[:-2], refs[-2:]
    feat = x.shape[0]
    rows[...] = jnp.zeros_like(rows)
    rows[0:1, 0:feat] = mod[pl.ds((step * 3 + 2) * N_TP + ids[1], 1), :]
    gate = jnp.transpose(rows[...])[0:feat, 0:1]
    acc = own[...]
    for part in came:
        acc += part[...].astype(F32)
    out[...] = (x[...].astype(F32) + gate * acc).astype(BF)


def swap(array):
    pairs = []
    for y in range(NY):
        for m in range(NH * NC):
            for l in range(NL):
                for x in range(NX):
                    here = (y * NX + m) * N_TP + l * NX + x
                    pairs.append((here, (y * NX + x) * N_TP + l * NX + m))
    return lax.ppermute(array, ("patch", "tp"), pairs)


def on_device(latent, modulation, stale_kv, w_qkv, w_out, q_gain, k_gain):
    tok, feat = latent.shape
    size = q_gain.shape[0]
    ids = jnp.stack([lax.axis_index("patch"), lax.axis_index("tp")]).astype(jnp.int32)
    mod = modulation.reshape(STEPS * 3 * N_TP, feat)
    qg, kg = q_gain.reshape(1, size), k_gain.reshape(1, size)
    x = latent.T

    def shape(*dims):
        return jax.ShapeDtypeStruct(dims, BF)

    def norm(step, groups):
        return call(
            functools.partial(norm_body, step),
            [shape(N_TP, feat, tok)],
            [ids, mod, *groups],
            [pltpu.VMEM((128, 256), F32)],
            4,
            8,
            "norm",
        )[0]

    rows_dev = w_qkv.shape[0]
    sent = w_qkv.reshape(rows_dev, 3, N_TP, size).transpose(2, 1, 0, 3).reshape(N_TP, 3 * rows_dev, size)
    cache = stale_kv.reshape(2 * tok, size)
    w_mine = lax.all_to_all(sent, "tp", 0, 0)
    x_l = shifts(x, "l", NL)
    cache_all = lax.all_gather(cache, "patch")
    w_back = swap(w_out)
    x, x_l, w_back, w_mine, ids, mod = sync(x, x_l, w_back, w_mine, ids, mod)
    w_mine = w_mine.reshape(N_TP, 3, rows_dev, size).transpose(0, 2, 1, 3).reshape(N_TP * rows_dev, 3 * size)
    w_mine = jnp.concatenate([w_mine, w_back], axis=1)
    w_h = shift(w_mine, "h", 1)
    x_four = jnp.stack([x] + x_l)
    x_up, x_down = shift(x_four, "x", 1), shift(x_four, "x", 3)
    w_h, x_up, x_down = sync(w_h, x_up, x_down)
    w_pair = jnp.stack([w_mine, w_h])
    w_up, w_down = shift(w_pair, "y", 1), shift(w_pair, "y", 3)
    x_far = shift(x_four, "x", 2)
    w_up, w_down, w_pair = sync(w_up, w_down, w_pair)
    w_far = [shift(w_up[:1], "y", 1), shift(w_down[1:], "y", 3)]
    w_quad = [w_pair, w_up, *w_far, w_down]
    w_c = [shift(piece, "c", 1) for piece in w_quad]
    normed = norm(0, [x_four, x_up, x_far, x_down])
    w_c, w_quad, normed = sync(w_c, w_quad, normed)
    past = cache_all
    weights = w_quad + w_c
    w_table = [place + NY * NH * kc for kc in range(NC) for place in (0, NH, 2 * NH, 2 * NH + 1, 3 * NH)]
    for step in range(STEPS):
        last = step + 1 == STEPS
        kv, near = call(
            functools.partial(qkv_body, w_table),
            [shape(2 * tok, size), shape(3 * tok, size)],
            [ids, normed, qg, kg, *weights],
            [],
            16,
            8,
            "qkv",
        )
        if not last:
            kv_all = lax.all_gather(kv, "patch")
        (attn,) = call(
            attend_body,
            [shape(size, tok)],
            [ids, near, past],
            [pltpu.VMEM((N_PATCH, tok, tok), F32)],
            8,
            12,
            "attend",
        )
        if not step:
            (w_all,) = call(
                functools.partial(arrange_body, w_table),
                [shape(NX * feat, NL * size)],
                [ids, *weights],
                [],
                3,
                8,
                "arrange",
            )
        came = shifts(attn, "l", NL)
        came, w_all = sync(came, w_all)
        own, *parts = call(
            partial_body,
            [jax.ShapeDtypeStruct((feat, tok), F32)] + [shape(feat, tok)] * (NX - 1),
            [ids, w_all, attn, *came],
            [pltpu.VMEM((NL * size, tok), BF)],
            2,
            8,
            "partial",
        )
        sums = [shift(part, "x", k + 1) for k, part in enumerate(parts)]
        (x,) = call(
            functools.partial(update_body, step),
            [shape(feat, tok)],
            [ids, mod, x, own, *sums],
            [pltpu.VMEM((128, 256), F32)],
            1,
            4,
            "update",
        )
        if last:
            break
        x_l = shifts(x, "l", NL)
        x_four = jnp.stack([x] + x_l)
        groups = [x_four] + shifts(x_four, "x", NX)
        normed = norm(step + 1, groups)
        past = kv_all
    return x.T, kv.reshape(2, tok, size)


def solution(mesh):
    in_specs = (
        P("patch", "tp"),
        P(),
        P(None, "patch", "tp"),
        P(("patch", "tp"), None, None),
        P("tp", "patch"),
        P(),
        P(),
    )
    out_specs = (P("patch", "tp"), P(None, "patch", "tp"))
    return jax.shard_map(on_device, mesh=mesh, in_specs=in_specs, out_specs=out_specs, check_vma=False)
```

```python
import functools

import jax
import jax.numpy as jnp
from jax import lax
from jax.experimental import pallas as pl
from jax.experimental.pallas import tpu as pltpu
from jax.sharding import PartitionSpec as P

NY, NH, NC = 4, 2, 2
NL, NX = 4, 4
N_TP = NL * NX
N_PATCH = NY * NH * NC
STEPS = 2
EPS = 1e-06
BF = jnp.bfloat16
F32 = jnp.float32
LOG2E = 1.4426950408889634


def shift(array, axis, amount):
    if axis in ("l", "x"):
        pairs = []
        for l in range(NL):
            for x in range(NX):
                to = ((l + amount) % NL, x) if axis == "l" else (l, (x + amount) % NX)
                pairs.append((l * NX + x, to[0] * NX + to[1]))
        return lax.ppermute(array, "tp", pairs)
    pairs = []
    for y in range(NY):
        for h in range(NH):
            for c in range(NC):
                to = {
                    "y": ((y + amount) % NY, h, c),
                    "h": (y, (h + amount) % NH, c),
                    "c": (y, h, (c + amount) % NC),
                }[axis]
                pairs.append(((y * NH + h) * NC + c, (to[0] * NH + to[1]) * NC + to[2]))
    return lax.ppermute(array, "patch", pairs)


def shifts(array, axis, count):
    return [shift(array, axis, k) for k in range(1, count)]


def sync(*trees):
    leaves, kind = jax.tree.flatten(trees)
    return jax.tree.unflatten(kind, lax.optimization_barrier(tuple(leaves)))


def call(body, outs, inputs, scratch, cost, room, name):
    vector = pl.BlockSpec(memory_space=pltpu.VMEM)
    return pl.pallas_call(
        body,
        out_shape=outs,
        in_specs=[pl.BlockSpec(memory_space=pltpu.SMEM)] + [vector] * (len(inputs) - 1),
        out_specs=[vector] * len(outs),
        scratch_shapes=scratch,
        compiler_params=pltpu.CompilerParams(vmem_limit_bytes=room << 20),
        cost_estimate=pl.CostEstimate(flops=1 << 20, bytes_accessed=cost << 20, transcendentals=0),
        name=name,
    )(*inputs)


def dot(a, b, dims):
    return lax.dot_general(a, b, (dims, ((), ())), preferred_element_type=F32)


def blocks(refs, table):
    return [(ref, i, first + i) for ref, first in zip(refs, table) for i in range(ref.shape[0])]


def tp_of(ids, n):
    l, x = ids[1] // NX, ids[1] % NX
    return ((l + NL - n % NL) % NL) * NX + (x + NX - n // NL) % NX


def patch_of(ids, n):
    patch = ids[0]
    y, h, c = patch // (NH * NC), (patch // NC) % NH, patch % NC
    ky, kh, kc = (n // NH) % NY, n % NH, n // (NH * NY)
    return (((y + NY - ky) % NY) * NH + (h + kh) % NH) * NC + (c + kc) % NC


def norm_body(step, ids, mod, *refs):
    groups, (normed, rows) = refs[:NX], refs[NX:]
    feat, tok = normed.shape[1:]
    total = feat * N_TP
    places = blocks(groups, [NL * k for k in range(NX)])
    rows[...] = jnp.zeros_like(rows)
    for n in range(N_TP):
        t = tp_of(ids, n)
        rows[n : n + 1, 0:feat] = mod[pl.ds((step * 3 + 1) * N_TP + t, 1), :] + 1.0
        rows[n + 16 : n + 17, 0:feat] = mod[pl.ds(step * 3 * N_TP + t, 1), :]
    cols = jnp.transpose(rows[...])
    mean = jnp.zeros((1, tok), F32)
    for ref, i, n in places:
        mean += jnp.sum(ref[i].astype(F32), axis=0, keepdims=True)
    mean = mean / total
    spread = jnp.zeros((1, tok), F32)
    for ref, i, n in places:
        centre = ref[i].astype(F32) - mean
        spread += jnp.sum(centre * centre, axis=0, keepdims=True)
    rstd = lax.rsqrt(spread / total + EPS)
    for ref, i, n in places:
        block = (ref[i].astype(F32) - mean) * rstd
        block = block * cols[0:feat, n : n + 1] + cols[0:feat, n + 16 : n + 17]
        normed[tp_of(ids, n)] = block.astype(BF)


def qkv_body(table, ids, normed, qg, kg, *refs):
    weights, (kv_out, near) = refs[: len(table)], refs[len(table) :]
    tok, size = normed.shape[2], qg.shape[-1]
    qkv = jnp.zeros((tok, 3 * size), F32)
    for ref, i, n in blocks(weights, table):
        qkv += dot(normed[patch_of(ids, n)], ref[i, :, 0 : 3 * size], ((0,), (0,)))
    for n, gain in enumerate((qg, kg)):
        one = qkv[:, n * size : (n + 1) * size]
        scale = lax.rsqrt(jnp.mean(one * one, axis=-1, keepdims=True) + EPS)
        near[n * tok : (n + 1) * tok] = (one * scale * gain[...]).astype(BF)
    near[2 * tok :] = qkv[:, 2 * size :].astype(BF)
    kv_out[...] = near[tok:]


def attend_body(ids, near, past, out, scores):
    tok, size = near.shape[0] // 3, near.shape[1]

    def block(n, rows):
        own = near[tok + rows.start : tok + rows.stop]
        return jnp.where(ids[0] == n, own, past[n, rows])

    q = near[0:tok]
    top = jnp.full((1, tok), -jnp.inf, F32)
    for n in range(N_PATCH):
        part = dot(block(n, slice(0, tok)), q, ((1,), (1,)))
        scores[n] = part
        top = jnp.maximum(top, jnp.max(part, axis=0, keepdims=True))
    inv = LOG2E / size**0.5
    total = jnp.zeros((1, tok), F32)
    mixed = jnp.zeros((size, tok), F32)
    for n in range(N_PATCH):
        p = jnp.exp2((scores[n] - top) * inv)
        total += jnp.sum(p, axis=0, keepdims=True)
        mixed += dot(block(n, slice(tok, 2 * tok)), p.astype(BF), ((0,), (0,)))
    out[...] = (mixed / total).astype(BF)


def arrange_body(table, ids, *refs):
    weights, out = refs[:-1], refs[-1]
    size = out.shape[1] // NL
    feat = out.shape[0] // NX
    l, x = ids[1] // NX, ids[1] % NX
    for ref, i, n in blocks(weights, table):
        patch = patch_of(ids, n)
        k = (patch % NX + NX - x) % NX
        kl = (l + NL - patch // NX) % NL
        rows = pl.ds(pl.multiple_of(k * feat, feat), feat)
        lanes = pl.ds(pl.multiple_of(kl * size, size), size)
        out[rows, lanes] = ref[i, :, 3 * size :]


def partial_body(ids, weights, *refs):
    attn, outs, mixed = refs[:NL], refs[NL:-1], refs[-1]
    size, feat = attn[0].shape[0], outs[0].shape[0]
    for n, part in enumerate(attn):
        mixed[n * size : (n + 1) * size] = part[...]
    acc = dot(weights[...], mixed[...], ((1,), (0,)))
    for n, out in enumerate(outs):
        out[...] = acc[n * feat : (n + 1) * feat].astype(out.dtype)


def update_body(step, ids, mod, x, own, *refs):
    came, (out, rows) = refs[:-2], refs[-2:]
    feat = x.shape[0]
    rows[...] = jnp.zeros_like(rows)
    rows[0:1, 0:feat] = mod[pl.ds((step * 3 + 2) * N_TP + ids[1], 1), :]
    gate = jnp.transpose(rows[...])[0:feat, 0:1]
    acc = own[...]
    for part in came:
        acc += part[...].astype(F32)
    out[...] = (x[...].astype(F32) + gate * acc).astype(BF)


def swap(array):
    pairs = []
    for y in range(NY):
        for m in range(NH * NC):
            for l in range(NL):
                for x in range(NX):
                    here = (y * NX + m) * N_TP + l * NX + x
                    pairs.append((here, (y * NX + x) * N_TP + l * NX + m))
    return lax.ppermute(array, ("patch", "tp"), pairs)


def on_device(latent, modulation, stale_kv, w_qkv, w_out, q_gain, k_gain):
    tok, feat = latent.shape
    size = q_gain.shape[0]
    ids = jnp.stack([lax.axis_index("patch"), lax.axis_index("tp")]).astype(jnp.int32)
    mod = modulation.reshape(STEPS * 3 * N_TP, feat)
    qg, kg = q_gain.reshape(1, size), k_gain.reshape(1, size)
    x = latent.T

    def shape(*dims):
        return jax.ShapeDtypeStruct(dims, BF)

    def norm(step, groups):
        return call(
            functools.partial(norm_body, step),
            [shape(N_TP, feat, tok)],
            [ids, mod, *groups],
            [pltpu.VMEM((128, 256), F32)],
            4,
            8,
            "norm",
        )[0]

    rows_dev = w_qkv.shape[0]
    sent = w_qkv.reshape(rows_dev, 3, N_TP, size).transpose(2, 1, 0, 3).reshape(N_TP, 3 * rows_dev, size)
    cache = stale_kv.reshape(2 * tok, size)
    w_mine = lax.all_to_all(sent, "tp", 0, 0)
    x_l = shifts(x, "l", NL)
    cache_all = lax.all_gather(cache, "patch")
    w_back = swap(w_out)
    x, x_l, w_back, w_mine, ids, mod = sync(x, x_l, w_back, w_mine, ids, mod)
    w_mine = w_mine.reshape(N_TP, 3, rows_dev, size).transpose(0, 2, 1, 3).reshape(N_TP * rows_dev, 3 * size)
    w_mine = jnp.concatenate([w_mine, w_back], axis=1)
    w_h = shift(w_mine, "h", 1)
    x_four = jnp.stack([x] + x_l)
    x_up, x_down = shift(x_four, "x", 1), shift(x_four, "x", 3)
    w_h, x_up, x_down = sync(w_h, x_up, x_down)
    w_pair = jnp.stack([w_mine, w_h])
    w_up, w_down = shift(w_pair, "y", 1), shift(w_pair, "y", 3)
    x_far = shift(x_four, "x", 2)
    w_up, w_down, w_pair = sync(w_up, w_down, w_pair)
    w_far = [shift(w_up[:1], "y", 1), shift(w_down[1:], "y", 3)]
    w_quad = [w_pair, w_up, *w_far, w_down]
    normed = norm(0, [x_four, x_up, x_far, x_down])
    ready = [w_pair, w_up, *(sync(piece, normed)[0] for piece in w_far), w_down]
    w_c = [shift(piece, "c", 1) for piece in ready]
    w_c, w_quad, normed = sync(w_c, w_quad, normed)
    past = cache_all
    weights = w_quad + w_c
    w_table = [place + NY * NH * kc for kc in range(NC) for place in (0, NH, 2 * NH, 2 * NH + 1, 3 * NH)]
    for step in range(STEPS):
        last = step + 1 == STEPS
        kv, near = call(
            functools.partial(qkv_body, w_table),
            [shape(2 * tok, size), shape(3 * tok, size)],
            [ids, normed, qg, kg, *weights],
            [],
            16,
            8,
            "qkv",
        )
        if not last:
            kv_all = lax.all_gather(kv, "patch")
        (attn,) = call(
            attend_body,
            [shape(size, tok)],
            [ids, near, past],
            [pltpu.VMEM((N_PATCH, tok, tok), F32)],
            8,
            12,
            "attend",
        )
        if not step:
            (w_all,) = call(
                functools.partial(arrange_body, w_table),
                [shape(NX * feat, NL * size)],
                [ids, *weights],
                [],
                3,
                8,
                "arrange",
            )
        came = shifts(attn, "l", NL)
        came, w_all = sync(came, w_all)
        own, *parts = call(
            partial_body,
            [jax.ShapeDtypeStruct((feat, tok), F32)] + [shape(feat, tok)] * (NX - 1),
            [ids, w_all, attn, *came],
            [pltpu.VMEM((NL * size, tok), BF)],
            2,
            8,
            "partial",
        )
        sums = [shift(part, "x", k + 1) for k, part in enumerate(parts)]
        (x,) = call(
            functools.partial(update_body, step),
            [shape(feat, tok)],
            [ids, mod, x, own, *sums],
            [pltpu.VMEM((128, 256), F32)],
            1,
            4,
            "update",
        )
        if last:
            break
        x_l = shifts(x, "l", NL)
        x_four = jnp.stack([x] + x_l)
        groups = [x_four] + shifts(x_four, "x", NX)
        normed = norm(step + 1, groups)
        past = kv_all
    return x.T, kv.reshape(2, tok, size)


def solution(mesh):
    in_specs = (
        P("patch", "tp"),
        P(),
        P(None, "patch", "tp"),
        P(("patch", "tp"), None, None),
        P("tp", "patch"),
        P(),
        P(),
    )
    out_specs = (P("patch", "tp"), P(None, "patch", "tp"))
    return jax.shard_map(on_device, mesh=mesh, in_specs=in_specs, out_specs=out_specs, check_vma=False)
```

```python
import functools

import jax
import jax.numpy as jnp
from jax import lax
from jax.experimental import pallas as pl
from jax.experimental.pallas import tpu as pltpu
from jax.sharding import PartitionSpec as P

NY, NH, NC = 4, 2, 2
NL, NX = 4, 4
N_TP = NL * NX
N_PATCH = NY * NH * NC
STEPS = 2
EPS = 1e-06
BF = jnp.bfloat16
F32 = jnp.float32
LOG2E = 1.4426950408889634


def shift(array, axis, amount):
    if axis in ("l", "x"):
        pairs = []
        for l in range(NL):
            for x in range(NX):
                to = ((l + amount) % NL, x) if axis == "l" else (l, (x + amount) % NX)
                pairs.append((l * NX + x, to[0] * NX + to[1]))
        return lax.ppermute(array, "tp", pairs)
    pairs = []
    for y in range(NY):
        for h in range(NH):
            for c in range(NC):
                to = {
                    "y": ((y + amount) % NY, h, c),
                    "h": (y, (h + amount) % NH, c),
                    "c": (y, h, (c + amount) % NC),
                }[axis]
                pairs.append(((y * NH + h) * NC + c, (to[0] * NH + to[1]) * NC + to[2]))
    return lax.ppermute(array, "patch", pairs)


def shifts(array, axis, count):
    return [shift(array, axis, k) for k in range(1, count)]


def sync(*trees):
    leaves, kind = jax.tree.flatten(trees)
    return jax.tree.unflatten(kind, lax.optimization_barrier(tuple(leaves)))


def call(body, outs, inputs, scratch, cost, room, name):
    vector = pl.BlockSpec(memory_space=pltpu.VMEM)
    return pl.pallas_call(
        body,
        out_shape=outs,
        in_specs=[pl.BlockSpec(memory_space=pltpu.SMEM)] + [vector] * (len(inputs) - 1),
        out_specs=[vector] * len(outs),
        scratch_shapes=scratch,
        compiler_params=pltpu.CompilerParams(vmem_limit_bytes=room << 20),
        cost_estimate=pl.CostEstimate(flops=1 << 20, bytes_accessed=cost << 20, transcendentals=0),
        name=name,
    )(*inputs)


def dot(a, b, dims):
    return lax.dot_general(a, b, (dims, ((), ())), preferred_element_type=F32)


def blocks(refs, table):
    return [(ref, i, first + i) for ref, first in zip(refs, table) for i in range(ref.shape[0])]


def tp_of(ids, n):
    l, x = ids[1] // NX, ids[1] % NX
    return ((l + NL - n % NL) % NL) * NX + (x + NX - n // NL) % NX


def patch_of(ids, n):
    patch = ids[0]
    y, h, c = patch // (NH * NC), (patch // NC) % NH, patch % NC
    ky, kh, kc = (n // NH) % NY, n % NH, n // (NH * NY)
    return (((y + NY - ky) % NY) * NH + (h + kh) % NH) * NC + (c + kc) % NC


def norm_body(step, ids, mod, *refs):
    groups, (normed, rows) = refs[:NX], refs[NX:]
    feat, tok = normed.shape[1:]
    total = feat * N_TP
    places = blocks(groups, [NL * k for k in range(NX)])
    rows[...] = jnp.zeros_like(rows)
    for n in range(N_TP):
        t = tp_of(ids, n)
        rows[n : n + 1, 0:feat] = mod[pl.ds((step * 3 + 1) * N_TP + t, 1), :] + 1.0
        rows[n + 16 : n + 17, 0:feat] = mod[pl.ds(step * 3 * N_TP + t, 1), :]
    cols = jnp.transpose(rows[...])
    mean = jnp.zeros((1, tok), F32)
    for ref, i, n in places:
        mean += jnp.sum(ref[i].astype(F32), axis=0, keepdims=True)
    mean = mean / total
    spread = jnp.zeros((1, tok), F32)
    for ref, i, n in places:
        centre = ref[i].astype(F32) - mean
        spread += jnp.sum(centre * centre, axis=0, keepdims=True)
    rstd = lax.rsqrt(spread / total + EPS)
    for ref, i, n in places:
        block = (ref[i].astype(F32) - mean) * rstd
        block = block * cols[0:feat, n : n + 1] + cols[0:feat, n + 16 : n + 17]
        normed[tp_of(ids, n)] = block.astype(BF)


def qkv_body(table, ids, normed, qg, kg, *refs):
    weights, (kv_out, near) = refs[: len(table)], refs[len(table) :]
    tok, size = normed.shape[2], qg.shape[-1]
    qkv = jnp.zeros((tok, 3 * size), F32)
    for ref, i, n in blocks(weights, table):
        qkv += dot(normed[patch_of(ids, n)], ref[i, :, 0 : 3 * size], ((0,), (0,)))
    for n, gain in enumerate((qg, kg)):
        one = qkv[:, n * size : (n + 1) * size]
        scale = lax.rsqrt(jnp.mean(one * one, axis=-1, keepdims=True) + EPS)
        near[n * tok : (n + 1) * tok] = (one * scale * gain[...]).astype(BF)
    near[2 * tok :] = qkv[:, 2 * size :].astype(BF)
    kv_out[...] = near[tok:]


def attend_body(ids, near, past, out, scores):
    tok, size = near.shape[0] // 3, near.shape[1]

    def block(n, rows):
        own = near[tok + rows.start : tok + rows.stop]
        return jnp.where(ids[0] == n, own, past[n, rows])

    q = near[0:tok]
    top = jnp.full((1, tok), -jnp.inf, F32)
    for n in range(N_PATCH):
        part = dot(block(n, slice(0, tok)), q, ((1,), (1,)))
        scores[n] = part
        top = jnp.maximum(top, jnp.max(part, axis=0, keepdims=True))
    inv = LOG2E / size**0.5
    total = jnp.zeros((1, tok), F32)
    mixed = jnp.zeros((size, tok), F32)
    for n in range(N_PATCH):
        p = jnp.exp2((scores[n] - top) * inv)
        total += jnp.sum(p, axis=0, keepdims=True)
        mixed += dot(block(n, slice(tok, 2 * tok)), p.astype(BF), ((0,), (0,)))
    out[...] = (mixed / total).astype(BF)


def arrange_body(table, ids, *refs):
    weights, out = refs[:-1], refs[-1]
    size = out.shape[1] // NL
    feat = out.shape[0] // NX
    l, x = ids[1] // NX, ids[1] % NX
    for ref, i, n in blocks(weights, table):
        patch = patch_of(ids, n)
        k = (patch % NX + NX - x) % NX
        kl = (l + NL - patch // NX) % NL
        rows = pl.ds(pl.multiple_of(k * feat, feat), feat)
        lanes = pl.ds(pl.multiple_of(kl * size, size), size)
        out[rows, lanes] = ref[i, :, 3 * size :]


def partial_body(ids, weights, *refs):
    attn, outs, mixed = refs[:NL], refs[NL:-1], refs[-1]
    size, feat = attn[0].shape[0], outs[0].shape[0]
    for n, part in enumerate(attn):
        mixed[n * size : (n + 1) * size] = part[...]
    acc = dot(weights[...], mixed[...], ((1,), (0,)))
    for n, out in enumerate(outs):
        out[...] = acc[n * feat : (n + 1) * feat].astype(out.dtype)


def update_body(step, ids, mod, x, own, *refs):
    came, (out, rows) = refs[:-2], refs[-2:]
    feat = x.shape[0]
    rows[...] = jnp.zeros_like(rows)
    rows[0:1, 0:feat] = mod[pl.ds((step * 3 + 2) * N_TP + ids[1], 1), :]
    gate = jnp.transpose(rows[...])[0:feat, 0:1]
    acc = own[...]
    for part in came:
        acc += part[...].astype(F32)
    out[...] = (x[...].astype(F32) + gate * acc).astype(BF)


def swap(array):
    pairs = []
    for y in range(NY):
        for m in range(NH * NC):
            for l in range(NL):
                for x in range(NX):
                    here = (y * NX + m) * N_TP + l * NX + x
                    pairs.append((here, (y * NX + x) * N_TP + l * NX + m))
    return lax.ppermute(array, ("patch", "tp"), pairs)


def on_device(latent, modulation, stale_kv, w_qkv, w_out, q_gain, k_gain):
    tok, feat = latent.shape
    size = q_gain.shape[0]
    ids = jnp.stack([lax.axis_index("patch"), lax.axis_index("tp")]).astype(jnp.int32)
    mod = modulation.reshape(STEPS * 3 * N_TP, feat)
    qg, kg = q_gain.reshape(1, size), k_gain.reshape(1, size)
    x = latent.T

    def shape(*dims):
        return jax.ShapeDtypeStruct(dims, BF)

    def norm(step, groups):
        return call(
            functools.partial(norm_body, step),
            [shape(N_TP, feat, tok)],
            [ids, mod, *groups],
            [pltpu.VMEM((128, 256), F32)],
            4,
            8,
            "norm",
        )[0]

    rows_dev = w_qkv.shape[0]
    sent = w_qkv.reshape(rows_dev, 3, N_TP, size).transpose(2, 1, 0, 3).reshape(N_TP, 3 * rows_dev, size)
    cache = stale_kv.reshape(2 * tok, size)
    w_mine = lax.all_to_all(sent, "tp", 0, 0)
    x_l = shifts(x, "l", NL)
    cache_all = lax.all_gather(cache, "patch")
    w_back = swap(w_out)
    x, x_l, w_back, w_mine, ids, mod = sync(x, x_l, w_back, w_mine, ids, mod)
    w_mine = w_mine.reshape(N_TP, 3, rows_dev, size).transpose(0, 2, 1, 3).reshape(N_TP * rows_dev, 3 * size)
    w_mine = jnp.concatenate([w_mine, w_back], axis=1)
    w_h = shift(w_mine, "h", 1)
    x_four = jnp.stack([x] + x_l)
    x_up, x_down = shift(x_four, "x", 1), shift(x_four, "x", 3)
    w_h, x_up, x_down = sync(w_h, x_up, x_down)
    w_pair = jnp.stack([w_mine, w_h])
    w_up, w_down = shift(w_pair, "y", 1), shift(w_pair, "y", 3)
    x_far = shift(x_four, "x", 2)
    w_up, w_down, w_pair = sync(w_up, w_down, w_pair)
    w_far = [shift(w_up[:1], "y", 1), shift(w_down[1:], "y", 3)]
    w_quad = [w_pair, w_up, *w_far, w_down]
    w_c = [shift(piece, "c", 1) for piece in w_quad]
    normed = norm(0, [x_four, x_up, x_far, x_down])
    w_c, w_quad, normed = sync(w_c, w_quad, normed)
    past = cache_all
    weights = w_quad + w_c
    w_table = [place + NY * NH * kc for kc in range(NC) for place in (0, NH, 2 * NH, 2 * NH + 1, 3 * NH)]
    for step in range(STEPS):
        last = step + 1 == STEPS
        kv, near = call(
            functools.partial(qkv_body, w_table),
            [shape(2 * tok, size), shape(3 * tok, size)],
            [ids, normed, qg, kg, *weights],
            [],
            16,
            8,
            "qkv",
        )
        if not last:
            kv_all = lax.all_gather(kv, "patch")
        (attn,) = call(
            attend_body,
            [shape(size, tok)],
            [ids, near, past],
            [pltpu.VMEM((N_PATCH, tok, tok), F32)],
            8,
            12,
            "attend",
        )
        if not step:
            (w_all,) = call(
                functools.partial(arrange_body, w_table),
                [shape(NX * feat, NL * size)],
                [ids, *weights],
                [],
                3,
                8,
                "arrange",
            )
        came = shifts(attn, "l", NL)
        came, w_all = sync(came, w_all)
        own, *parts = call(
            partial_body,
            [jax.ShapeDtypeStruct((feat, tok), F32)] + [shape(feat, tok)] * (NX - 1),
            [ids, w_all, attn, *came],
            [pltpu.VMEM((NL * size, tok), BF)],
            2,
            8,
            "partial",
        )
        sums = [shift(part, "x", k + 1) for k, part in enumerate(parts)]
        (x,) = call(
            functools.partial(update_body, step),
            [shape(feat, tok)],
            [ids, mod, x, own, *sums],
            [pltpu.VMEM((128, 256), F32)],
            1,
            4,
            "update",
        )
        if last:
            break
        x_l = shifts(x, "l", NL)
        x_four = jnp.stack([x] + x_l)
        x_up, x_down = shift(x_four, "x", 1), shift(x_four, "x", 3)
        x_up, x_down, x_four = sync(x_up, x_down, x_four)
        half = NL // 2
        x_far = jnp.concatenate([shift(x_up[:half], "x", 1), shift(x_down[half:], "x", 3)])
        groups = [x_four, x_up, x_far, x_down]
        normed = norm(step + 1, groups)
        past = kv_all
    return x.T, kv.reshape(2, tok, size)


def solution(mesh):
    in_specs = (
        P("patch", "tp"),
        P(),
        P(None, "patch", "tp"),
        P(("patch", "tp"), None, None),
        P("tp", "patch"),
        P(),
        P(),
    )
    out_specs = (P("patch", "tp"), P(None, "patch", "tp"))
    return jax.shard_map(on_device, mesh=mesh, in_specs=in_specs, out_specs=out_specs, check_vma=False)
```
